32 devices in a mesh: box: 32 (over z, y, x, core), exc: 1.
Axes of the slice: x: 2, y: 2, z: 4, core: 2. Of those that a mesh axis runs over, the one named last changes fastest.
Arguments:
- incident: bfloat16 [2, 2, 128, 512], P(None, 'exc', 'box'), may hold values from -7 to 7
- contrast: int32 [128, 512], P('box'), may hold values from 1 to 16
- box_pos: int32 [128], replicated, may hold values from 0 to 3, as said below
- directions: float32 [3, 512], P(None, 'box'), may hold values from -1 to 1, as said below
- enc_table: bfloat16 [2, 512, 512], replicated, may hold values from -0.25 to 0.25
- dec_table: bfloat16 [2, 512, 512], replicated, may hold values from -0.25 to 0.25
Outputs:
- scattered_one: bfloat16 [2, 2, 128, 512], P(None, 'exc', 'box')
- scattered_two: bfloat16 [2, 2, 128, 512], P(None, 'exc', 'box')
- series_ratio: float32 [128], P('box')
The draws below stay inside these ranges and needn't reach their ends.
Inputs may be any that keep to these rules, and one draw needn't show every extreme that they name: `box_pos`: entries 4 m to 4 m + 3 hold each number from 0 to 3 once. `directions`: each column is a unit vector.
All inputs are finite; a program needn't handle non-finite values.
Results may differ from the reference program's by a relative error of at most 0.0053.
Values may be sent and summed in bfloat16 or wider, within the bound.
A program may use at most 128 MiB of HBM per device.

```python
import math
import jax
import jax.numpy as jnp
from jax import lax

BSIDE = 8
CY = 2
CZ = 2
K = 512
V = 512
BOX_DEV = 4
BOXES = 128
EXC = 2


def draw_incident(key, part):
    ramp = jnp.arange(EXC, dtype=jnp.float32) / max(EXC - 1, 1)
    values = jnp.clip(jax.random.normal(key, (2, EXC, BOXES, V), jnp.float32), -4.0, 4.0)
    amplitude = 3.0 ** (ramp - 0.5)
    return (values * amplitude[None, :, None, None]).astype(jnp.bfloat16)


def permute_slab(subkey):
    return jax.random.permutation(subkey, CY * CZ)


def draw_box_pos(key, part):
    slab_count = BOXES // (CY * CZ)
    key_list = jax.random.split(key, slab_count)
    return jax.vmap(permute_slab)(key_list).reshape(BOXES).astype(jnp.int32)


def draw_directions(key, part):
    first_key, second_key = jax.random.split(jax.random.fold_in(key, 7))
    height = jax.random.uniform(first_key, (K,), jnp.float32, -1.0, 1.0)
    azimuth = jax.random.uniform(second_key, (K,), jnp.float32, -math.pi, math.pi)
    beside_all = jnp.sqrt(jnp.maximum(1.0 - height * height, 0.0))
    return jnp.stack([beside_all * jnp.cos(azimuth), beside_all * jnp.sin(azimuth), height]).astype(jnp.float32)


def touch_ends(array, own_key, low, largest):
    place = [jax.random.randint(jax.random.fold_in(own_key, axis), (), 0, length) for axis, length in enumerate(array.shape)]
    widest = array.shape.index(max(array.shape))
    neighbour = place[:widest] + [(place[widest] + 1) % array.shape[widest]] + place[widest + 1:]
    return array.at[tuple(place)].set(low).at[tuple(neighbour)].set(largest)


def normal_values(stream_key, dims, deviation, bound, held_as=jnp.bfloat16):
    return jnp.clip(deviation * jax.random.normal(stream_key, dims, jnp.float32), -bound, bound).astype(held_as)


def setup_inputs(seed: int = 0) -> dict:
    streams_of = jax.random.split(jax.random.key(seed), 7)
    return {
        "incident": draw_incident(jax.random.fold_in(streams_of[6], 71), 0),
        "contrast": touch_ends(jax.random.randint(streams_of[1], (BOXES, V), 1, 17), jax.random.fold_in(streams_of[1], 1), 1, 16).astype(jnp.int32),
        "box_pos": draw_box_pos(jax.random.fold_in(streams_of[6], 71), 0),
        "directions": draw_directions(jax.random.fold_in(streams_of[6], 71), 0),
        "enc_table": normal_values(streams_of[4], (2, K, V), V ** -0.5, 0.25),
        "dec_table": normal_values(streams_of[5], (2, V, K), K ** -0.5, 0.25),
    }


wave_number = 0.8
near_scale = 0.1
self_value = 1.0
far_scale = 0.25
chi_step = 0.0625
epsilon = 1e-06

def voxel_axes():
    voxel_index = jnp.arange(BSIDE ** 3, dtype=jnp.int32)
    return (voxel_index // (BSIDE * BSIDE), voxel_index // BSIDE % BSIDE, voxel_index % BSIDE)

def green_block(offset):
    coords = voxel_axes()
    square = jnp.zeros((BSIDE ** 3, BSIDE ** 3), jnp.int32)
    for dimension in range(3):
        differ = coords[dimension][:, None] - coords[dimension][None, :] - BSIDE * offset[dimension]
        square = square + differ * differ
    square = square.astype(jnp.float32)
    radius = jnp.sqrt(jnp.maximum(square, 1.0))
    inside = square < 0.5
    real_part = jnp.where(inside, self_value, near_scale * jnp.cos(wave_number * radius) / radius)
    imag_part = jnp.where(inside, 0.0, near_scale * jnp.sin(wave_number * radius) / radius)
    return jnp.stack([real_part, imag_part]).astype(jnp.bfloat16)

def box_coords(box_pos):
    box_count = box_pos.shape[0]
    slab_coord = (jnp.arange(box_count, dtype=jnp.int32) // (CY * CZ)).astype(jnp.float32)
    row_coord = (box_pos // CZ).astype(jnp.float32)
    col_coord = (box_pos % CZ).astype(jnp.float32)
    return (slab_coord, row_coord, col_coord)

def translator(column, coords):
    slab_gap = coords[0][:, None] - coords[0][None, :]
    row_gap = coords[1][:, None] - coords[1][None, :]
    col_gap = coords[2][:, None] - coords[2][None, :]
    square = slab_gap * slab_gap + row_gap * row_gap + col_gap * col_gap
    nearby = jnp.maximum(jnp.maximum(jnp.abs(slab_gap), jnp.abs(row_gap)), jnp.abs(col_gap)) < 1.5
    radius = jnp.sqrt(jnp.maximum(square, 1.0))
    kappa = wave_number * BSIDE
    argument = kappa * radius
    inverse = 1.0 / argument
    cosine = (column[0] * slab_gap + column[1] * row_gap + column[2] * col_gap) / radius
    prev_re, prev_im = (inverse, jnp.zeros_like(inverse))
    now_re, now_im = (jnp.zeros_like(inverse), -inverse)
    leg_prev, leg_now = (jnp.ones_like(inverse), jnp.ones_like(inverse))
    total_re = jnp.zeros_like(inverse)
    total_im = jnp.zeros_like(inverse)
    for order in range(4):
        if order == 0:
            legendre = jnp.ones_like(inverse)
        elif order == 1:
            legendre = cosine
        else:
            legendre = ((2 * order - 1) * cosine * leg_now - (order - 1) * leg_prev) / order
        leg_prev, leg_now = (leg_now, legendre)
        weight = (2.0 * order + 1.0) * legendre
        rot = order % 4
        if rot == 0:
            term_re, term_im = (now_re, now_im)
        elif rot == 1:
            term_re, term_im = (-now_im, now_re)
        elif rot == 2:
            term_re, term_im = (-now_re, -now_im)
        else:
            term_re, term_im = (now_im, -now_re)
        total_re = total_re + weight * term_re
        total_im = total_im + weight * term_im
        next_re = (2.0 * order + 1.0) * inverse * now_re - prev_re
        next_im = (2.0 * order + 1.0) * inverse * now_im - prev_im
        prev_re, prev_im = (now_re, now_im)
        now_re, now_im = (next_re, next_im)
    wave_re = jnp.cos(argument)
    wave_im = jnp.sin(argument)
    factor = jnp.where(nearby, 0.0, far_scale * kappa / 16.0)
    real_part = factor * (total_re * wave_re - total_im * wave_im)
    imag_part = factor * (total_re * wave_im + total_im * wave_re)
    return jnp.stack([real_part, imag_part]).astype(jnp.bfloat16)

def near_reference(sources, slots):
    slab_count = BOXES // BOX_DEV
    grid = jnp.zeros_like(sources).at[:, :, slots, :].set(sources)
    grid = grid.astype(jnp.float32).reshape(2, EXC, slab_count, CY, CZ, V)
    padded = jnp.pad(grid, ((0, 0), (0, 0), (1, 1), (0, 0), (0, 0), (0, 0)))
    accumulated = jnp.zeros((2, EXC, slab_count, CY, CZ, V), jnp.float32)
    for shift_x in (-1, 0, 1):
        for shift_y in (-1, 0, 1):
            for shift_z in (-1, 0, 1):
                row_low = max(0, -shift_y)
                row_high = CY - max(0, shift_y)
                col_low = max(0, -shift_z)
                col_high = CZ - max(0, shift_z)
                if row_high <= row_low or col_high <= col_low:
                    continue
                block = green_block((shift_x, shift_y, shift_z)).astype(jnp.float32)
                piece = padded[:, :, 1 + shift_x:1 + shift_x + slab_count, row_low + shift_y:row_high + shift_y, col_low + shift_z:col_high + shift_z, :]
                real_prod = jnp.einsum('xesyzj,ij->xesyzi', piece, block[0], precision=lax.Precision.HIGHEST)
                imag_prod = jnp.einsum('xesyzj,ij->xesyzi', piece, block[1], precision=lax.Precision.HIGHEST)
                update = jnp.stack([real_prod[0] - imag_prod[1], imag_prod[0] + real_prod[1]])
                accumulated = accumulated.at[:, :, :, row_low:row_high, col_low:col_high, :].add(update)
    return accumulated.reshape(2, EXC, BOXES, V)[:, :, slots, :]

def reference(incident, contrast, box_pos, directions, enc_table, dec_table):
    contrast_real = contrast.astype(jnp.float32) * chi_step
    coords = box_coords(box_pos)
    slots = jnp.arange(BOXES, dtype=jnp.int32) // BOX_DEV * BOX_DEV + box_pos
    enc_float = enc_table.astype(jnp.float32)
    dec_float = dec_table.astype(jnp.float32)
    fields = incident
    outputs = []
    for term_index in range(2):
        sources = (contrast_real[None, None] * fields.astype(jnp.float32)).astype(jnp.bfloat16)
        near_part = near_reference(sources, slots)
        source_float = sources.astype(jnp.float32)
        real_prod = jnp.einsum('kv,xebv->kxeb', enc_float[0], source_float, precision=lax.Precision.HIGHEST)
        imag_prod = jnp.einsum('kv,xebv->kxeb', enc_float[1], source_float, precision=lax.Precision.HIGHEST)
        encoded = jnp.stack([real_prod[:, 0] - imag_prod[:, 1], imag_prod[:, 0] + real_prod[:, 1]], axis=1).astype(jnp.bfloat16)

        def one_direction(packed):
            column, coefficients = packed
            block = translator(column, coords).astype(jnp.float32)
            values = coefficients.astype(jnp.float32)
            real_part = jnp.einsum('ts,xes->xet', block[0], values, precision=lax.Precision.HIGHEST)
            imag_part = jnp.einsum('ts,xes->xet', block[1], values, precision=lax.Precision.HIGHEST)
            return jnp.stack([real_part[0] - imag_part[1], imag_part[0] + real_part[1]]).astype(jnp.bfloat16)
        translated = lax.map(one_direction, (jnp.transpose(directions), encoded)).astype(jnp.float32)
        real_back = jnp.einsum('vk,kxeb->xebv', dec_float[0], translated, precision=lax.Precision.HIGHEST)
        imag_back = jnp.einsum('vk,kxeb->xebv', dec_float[1], translated, precision=lax.Precision.HIGHEST)
        far_part = jnp.stack([real_back[0] - imag_back[1], imag_back[0] + real_back[1]])
        fields = (near_part + far_part).astype(jnp.bfloat16)
        outputs.append(fields)
    first_mean = lax.optimization_barrier(jnp.mean(jnp.square(outputs[0].astype(jnp.float32)), axis=(0, 1, 3)))
    second_mean = lax.optimization_barrier(jnp.mean(jnp.square(outputs[1].astype(jnp.float32)), axis=(0, 1, 3)))
    series_ratio = jnp.sqrt(second_mean / (first_mean + epsilon))
    return (outputs[0], outputs[1], series_ratio)
```

```python
import functools

import jax
import jax.numpy as jnp
import ml_dtypes
import numpy as np
from jax import lax
from jax.experimental import pallas as pl
from jax.experimental.pallas import tpu as pltpu
from jax.sharding import PartitionSpec as P

BSIDE = 8
CY = 2
CZ = 2
BOX_DEV = CY * CZ
ROWS = 4 * BOX_DEV
LANES = 128
TERMS = 16
MESH = pl.DeviceIdType.MESH

wave_number = 0.8
near_scale = 0.1
self_value = 1.0
far_scale = 0.25
chi_step = 0.0625
epsilon = 1e-06

F32 = jnp.float32
BF16 = jnp.bfloat16


def harmonics(x, y, z):
    s3, s6, s10, s15 = 3.0**0.5, 6.0**0.5, 10.0**0.5, 15.0**0.5
    xx, yy, zz = x * x, y * y, z * z
    return [
        (0, x * 0.0 + 1.0),
        (1, x),
        (1, y),
        (1, z),
        (2, s3 * x * y),
        (2, s3 * y * z),
        (2, s3 * x * z),
        (2, 0.5 * (2.0 * zz - xx - yy)),
        (2, 0.5 * s3 * (xx - yy)),
        (3, 0.5 * z * (2.0 * zz - 3.0 * xx - 3.0 * yy)),
        (3, 0.25 * s6 * x * (4.0 * zz - xx - yy)),
        (3, 0.25 * s6 * y * (4.0 * zz - xx - yy)),
        (3, 0.5 * s15 * z * (xx - yy)),
        (3, s15 * x * y * z),
        (3, 0.25 * s10 * x * (xx - 3.0 * yy)),
        (3, 0.25 * s10 * y * (3.0 * xx - yy)),
    ]


def near_planes():
    slot = np.arange(BOX_DEV * BSIDE * BSIDE)
    box, inner = slot // (BSIDE * BSIDE), slot % (BSIDE * BSIDE)
    row = box // CZ * BSIDE + inner // BSIDE
    col = box % CZ * BSIDE + inner % BSIDE
    gap = np.arange(2 * BSIDE)[:, None, None]
    square = gap**2 + (row[:, None] - row[None]) ** 2 + (col[:, None] - col[None]) ** 2
    radius = np.sqrt(np.maximum(square, 1).astype(np.float64))
    wave = near_scale * np.exp(1j * wave_number * radius) / radius
    wave = np.where(square == 0, self_value, wave)
    return np.concatenate([wave.real, wave.imag], axis=2).astype(ml_dtypes.bfloat16)


def far_terms(slabs):
    lane = np.arange(slabs * 8)
    slab = lane // 16 * 2 + lane % 2
    box = lane // 4 % 4
    part = lane // 2 % 2
    coords = np.stack([slab, box // CZ, box % CZ]).astype(np.float64)
    gap = coords[:, None, :] - coords[:, :, None]
    nearby = np.abs(gap).max(0) < 1.5
    radius = np.sqrt(np.maximum((gap**2).sum(0), 1.0))
    kappa = wave_number * BSIDE
    arg = kappa * radius
    before, now = np.exp(1j * arg) / arg, -1j * np.exp(1j * arg) / arg
    radial = []
    for order in range(4):
        value = (2 * order + 1) * 1j**order * now * far_scale * kappa / 16.0
        radial.append(np.where(nearby, 0.0, value))
        before, now = now, (2 * order + 1) * now / arg - before
    source, target = part[:, None], part[None, :]
    out = np.empty((TERMS, slabs * 8, slabs * 8), ml_dtypes.bfloat16)
    for term, (order, value) in enumerate(harmonics(*(gap / radius))):
        h = radial[order] * value
        cross = np.where(source == 0, h.imag, -h.imag)
        out[term] = np.where(source == target, h.real, cross).astype(ml_dtypes.bfloat16)
    return out


def nt(left, right):
    return lax.dot_general(left, right, (((1,), (1,)), ((), ())), preferred_element_type=F32)


def nn(left, right):
    return lax.dot_general(left, right, (((1,), (0,)), ((), ())), preferred_element_type=F32)


def times_i(x):
    rows = x.shape[0]
    row = lax.broadcasted_iota(jnp.int32, x.shape, 0)
    return jnp.where(row // 2 % 2 == 0, -pltpu.roll(x, rows - 2, 0), pltpu.roll(x, 2, 0))


def kernel(
    n, kdev, kpad, single, inc_ref, con_ref, pos_ref, dir_ref, enc_hbm, dec_hbm, near_hbm, far_hbm,
    one_ref, two_ref, rat_ref,
    enc_v, dec_v, near_v, far_v, own_x, nbr_x, snd, rcv, side_s, side_r, flat,
    load_sem, send_sem, recv_sem, side_ss, side_rs,
):
    me = lax.axis_index("box")
    barrier = pltpu.get_barrier_semaphore()

    def greet(j, carry):
        pl.semaphore_signal(barrier, inc=1, device_id={"box": lax.rem(me + j, n)}, device_id_type=MESH)
        return carry

    lax.fori_loop(1, n, greet, 0)
    loads = [
        pltpu.make_async_copy(hbm, vmem, load_sem.at[i])
        for i, (hbm, vmem) in enumerate(
            ((enc_hbm, enc_v), (near_hbm, near_v), (far_hbm, far_v), (dec_hbm, dec_v))
        )
    ]
    for load in loads:
        load.start()

    row = lax.broadcasted_iota(jnp.int32, (ROWS, ROWS), 0)
    col = lax.broadcasted_iota(jnp.int32, (ROWS, ROWS), 1)

    def spread(index):
        out = jnp.zeros((ROWS, ROWS), jnp.int32)
        for b in range(BOX_DEV):
            out = jnp.where(index % 4 == b, pos_ref[me * BOX_DEV + b], out)
        return out

    to_grid = jnp.where((row % 4 == col // 4) & (spread(col) == row // 4), 1.0, 0.0).astype(BF16)
    from_grid = jnp.where((col % 4 == row // 4) & (spread(row) == col // 4), 1.0, 0.0).astype(BF16)
    pieces = [inc_ref[a, e].astype(F32) for a in range(2) for e in range(2)]
    field = nn(to_grid, jnp.concatenate(pieces, axis=0).astype(BF16))
    step = con_ref[...].astype(F32) * chi_step
    own_pick = jnp.where((spread(col) == row // 4) & (col < 4), 1.0, 0.0).astype(BF16)
    chi = nn(own_pick, jnp.concatenate([step, jnp.zeros((12, step.shape[1]), F32)], axis=0).astype(BF16))

    drow = lax.broadcasted_iota(jnp.int32, (kpad, kdev), 0)
    dcol = lax.broadcasted_iota(jnp.int32, (kpad, kdev), 1)
    column = [
        jnp.sum(jnp.where(drow == dcol, dir_ref[c : c + 1, :], 0.0), axis=1, keepdims=True)
        for c in range(3)
    ]
    weights = [jnp.concatenate([y, y], axis=0) for _, y in harmonics(*column)]

    lane = lax.broadcasted_iota(jnp.int32, (kpad, LANES), 1)
    even = lane % 2 == 0
    own_x[...] = jnp.zeros_like(own_x)
    nbr_x[...] = jnp.zeros_like(nbr_x)
    if kdev != kpad:
        snd[...] = jnp.zeros_like(snd)
    plane = BSIDE * BSIDE

    def near_sum(ext, low, high):
        total = jnp.zeros((32, 2 * near_v.shape[1]), F32)
        for d in range(low, high):
            if d == 0:
                total += nn(ext[64:96, :].astype(BF16), near_v[0])
            else:
                both = jnp.concatenate([ext[64 + 4 * d : 96 + 4 * d, :], ext[64 - 4 * d : 96 - 4 * d, :]], axis=0)
                got = nn(both.astype(BF16), near_v[d])
                total += got[:32] + got[32:]
        return total

    def exchange(phase):
        def send(j, carry):
            there = lax.rem(me + j, n)
            pltpu.make_async_remote_copy(
                src_ref=snd.at[phase, there],
                dst_ref=rcv.at[phase, me],
                send_sem=send_sem.at[phase],
                recv_sem=recv_sem.at[phase],
                device_id={"box": there},
                device_id_type=MESH,
            ).start()
            return carry

        lax.fori_loop(1, n, send, 0)
        rcv[phase, pl.ds(me, 1)] = snd[phase, pl.ds(me, 1)]

    def arrived(phase):
        part = rcv.at[phase, pl.ds(0, n - 1)]
        pltpu.make_async_copy(part, part, recv_sem.at[phase]).wait()

    sums = []
    for turn in range(2):
        source = (chi * field).astype(BF16).astype(F32)
        planes = jnp.concatenate(
            [
                jnp.concatenate(
                    [source[4 * g : 4 * g + 4, x * plane : (x + 1) * plane] for g in range(BOX_DEV)], axis=1
                )
                for x in range(BSIDE)
            ],
            axis=0,
        )
        own_x[64:96, :] = planes
        side_s[turn] = planes.astype(BF16)
        if turn == 0:
            pl.semaphore_wait(barrier, n - 1)
        sides = []
        for s, away in enumerate((1, n - 1)):
            sides.append(
                pltpu.make_async_remote_copy(
                    src_ref=side_s.at[turn],
                    dst_ref=side_r.at[turn, s],
                    send_sem=side_ss.at[turn, s],
                    recv_sem=side_rs.at[turn, s],
                    device_id={"box": lax.rem(me + away, n)},
                    device_id_type=MESH,
                )
            )
            sides[-1].start()
        if turn == 0:
            loads[0].wait()
        first = jnp.concatenate([source, jnp.zeros((LANES - ROWS, source.shape[1]), F32)], axis=0)
        second = jnp.concatenate([times_i(source), jnp.zeros((LANES - ROWS, source.shape[1]), F32)], axis=0)
        encoded = nt(enc_v[0], first.astype(BF16)) + nt(enc_v[1], second.astype(BF16))
        if kdev == kpad:
            snd[2 * turn] = encoded.reshape(n, kdev, LANES).astype(BF16)
        else:
            for d in range(n):
                snd[2 * turn, d, :kdev, :] = encoded[d * kdev : (d + 1) * kdev, :].astype(BF16)
        exchange(2 * turn)

        if turn == 0:
            loads[1].wait()
        near = near_sum(own_x, 0, BSIDE)

        arrived(2 * turn)
        columns = [[], []]
        for group in range(n // 16):
            sum0, sum1 = (jnp.zeros((kpad, LANES), F32) for _ in range(2))
            for pair in range(8):
                a = rcv[2 * turn, group * 16 + pair * 2].astype(F32)
                b = rcv[2 * turn, group * 16 + pair * 2 + 1].astype(F32)
                exc0 = jnp.where(even, a, pltpu.roll(b, 1, 1))
                exc1 = jnp.where(even, pltpu.roll(a, LANES - 1, 1), b)
                if pair:
                    exc0, exc1 = pltpu.roll(exc0, 16 * pair, 1), pltpu.roll(exc1, 16 * pair, 1)
                sum0, sum1 = sum0 + exc0, sum1 + exc1
            columns[0].append(sum0)
            columns[1].append(sum1)
        waves = jnp.concatenate([jnp.concatenate(c, axis=1) for c in columns], axis=0).astype(BF16)
        if turn == 0:
            loads[2].wait()
        moved = jnp.zeros((2 * kpad, n * 8), F32)
        for term in range(TERMS):
            moved += weights[term] * nn(waves, far_v[term])
        for group in range(n // 16):
            out0 = moved[:kpad, group * LANES : (group + 1) * LANES]
            out1 = moved[kpad:, group * LANES : (group + 1) * LANES]
            for pair in range(8):
                a, b = out0, out1
                if pair:
                    a, b = pltpu.roll(a, LANES - 16 * pair, 1), pltpu.roll(b, LANES - 16 * pair, 1)
                slab = group * 16 + pair * 2
                snd[2 * turn + 1, slab] = jnp.where(even, a, pltpu.roll(b, 1, 1)).astype(BF16)
                snd[2 * turn + 1, slab + 1] = jnp.where(even, pltpu.roll(a, LANES - 1, 1), b).astype(BF16)
        exchange(2 * turn + 1)

        for side in sides:
            side.wait()
        nbr_x[32:64, :] = jnp.where(me > 0, side_r[turn, 0].astype(F32), 0.0)
        nbr_x[96:128, :] = jnp.where(me < n - 1, side_r[turn, 1].astype(F32), 0.0)
        near = near + near_sum(nbr_x, 1, 2 * BSIDE)
        half = near.shape[1] // 2
        near = near[:, :half] + times_i(near[:, half:])
        near = jnp.concatenate(
            [
                jnp.concatenate(
                    [near[4 * x : 4 * x + 4, g * plane : (g + 1) * plane] for x in range(BSIDE)], axis=1
                )
                for g in range(BOX_DEV)
            ],
            axis=0,
        )

        arrived(2 * turn + 1)
        if kdev == kpad:
            back = rcv[2 * turn + 1].astype(F32).reshape(n * kdev, LANES)
        else:
            for d in range(n):
                flat[d * kdev : (d + 1) * kdev, :] = rcv[2 * turn + 1, d].astype(F32)[:kdev, :]
            back = flat[...]
        back = jnp.transpose(back)[:ROWS]
        if turn == 0:
            loads[3].wait()
        far = nt(back.astype(BF16), dec_v[0]) + nt(times_i(back).astype(BF16), dec_v[1])
        rounded = (near + far).astype(BF16)
        result = nn(from_grid, rounded)
        out_ref = one_ref if turn == 0 else two_ref
        for a in range(2):
            for e in range(2):
                start = (2 * a + e) * BOX_DEV
                out_ref[a, e] = result[start : start + BOX_DEV].astype(BF16)
        field = rounded.astype(F32)
        square = jnp.sum(result * result, axis=1, keepdims=True)
        sums.append(square[:4] + square[4:8] + square[8:12] + square[12:])

    for phase in range(4):
        part = snd.at[phase, pl.ds(0, n - 1)]
        pltpu.make_async_copy(part, part, send_sem.at[phase]).wait()

    count = 4 * inc_ref.shape[3]
    if single:
        values = [jnp.sqrt(sums[1] / count / (sums[0] / count + epsilon))]
    else:
        values = sums
    brow = lax.broadcasted_iota(jnp.int32, (BOX_DEV, 1), 0)
    for i, value in enumerate(values):
        for b in range(BOX_DEV):
            rat_ref[i * BOX_DEV + b] = jnp.sum(jnp.where(brow == b, value, 0.0))


def shards(incident, contrast, box_pos, directions, enc_table, dec_table):
    n = lax.axis_size("box")
    exc_axis = lax.axis_size("exc")
    single = exc_axis == 1
    kdev = directions.shape[1]
    kpad = max(kdev, 16)
    near_np, far_np = near_planes(), far_terms(n)
    vmem = pl.BlockSpec(memory_space=pltpu.VMEM)
    smem = pl.BlockSpec(memory_space=pltpu.SMEM)
    anyspace = pl.BlockSpec(memory_space=pl.ANY)
    width = near_np.shape[1]
    one, two, ratio = pl.pallas_call(
        functools.partial(kernel, n, kdev, kpad, single),
        out_shape=(
            jax.ShapeDtypeStruct(incident.shape, BF16),
            jax.ShapeDtypeStruct(incident.shape, BF16),
            jax.ShapeDtypeStruct((BOX_DEV if single else 2 * BOX_DEV,), F32),
        ),
        in_specs=[vmem, vmem, smem, vmem, anyspace, anyspace, anyspace, anyspace],
        out_specs=(vmem, vmem, smem),
        scratch_shapes=[
            pltpu.VMEM(enc_table.shape, BF16),
            pltpu.VMEM(dec_table.shape, BF16),
            pltpu.VMEM(near_np.shape, BF16),
            pltpu.VMEM(far_np.shape, BF16),
            pltpu.VMEM((160, width), F32),
            pltpu.VMEM((160, width), F32),
            pltpu.VMEM((4, n, kpad, LANES), BF16),
            pltpu.VMEM((4, n, kpad, LANES), BF16),
            pltpu.VMEM((2, 32, width), BF16),
            pltpu.VMEM((2, 2, 32, width), BF16),
            pltpu.VMEM((n * kdev, LANES), F32),
            pltpu.SemaphoreType.DMA((4,)),
            pltpu.SemaphoreType.DMA((4,)),
            pltpu.SemaphoreType.DMA((4,)),
            pltpu.SemaphoreType.DMA((2, 2)),
            pltpu.SemaphoreType.DMA((2, 2)),
        ],
        compiler_params=pltpu.CompilerParams(
            collective_id=0, has_side_effects=True, vmem_limit_bytes=56 * 1024 * 1024
        ),
    )(
        incident, contrast, box_pos, directions, enc_table, dec_table, jnp.asarray(near_np), jnp.asarray(far_np)
    )
    if not single:
        sums = lax.psum(ratio.reshape(2, BOX_DEV), "exc")
        count = 4 * incident.shape[3] * exc_axis
        ratio = jnp.sqrt(sums[1] / count / (sums[0] / count + epsilon))
    return one, two, ratio


def solution(mesh):
    placed = (P(None, "exc", "box", None), P("box", None), P(), P(None, "box"), P(), P())
    return jax.shard_map(
        shards,
        mesh=mesh,
        in_specs=placed,
        out_specs=(P(None, "exc", "box", None), P(None, "exc", "box", None), P("box")),
        check_vma=False,
    )
```

```python
import functools

import jax
import jax.numpy as jnp
import ml_dtypes
import numpy as np
from jax import lax
from jax.experimental import pallas as pl
from jax.experimental.pallas import tpu as pltpu
from jax.sharding import PartitionSpec as P

BSIDE = 8
CY = 2
CZ = 2
BOX_DEV = CY * CZ
ROWS = 4 * BOX_DEV
LANES = 128
TERMS = 16
MESH = pl.DeviceIdType.MESH

wave_number = 0.8
near_scale = 0.1
self_value = 1.0
far_scale = 0.25
chi_step = 0.0625
epsilon = 1e-06

F32 = jnp.float32
BF16 = jnp.bfloat16


def harmonics(x, y, z):
    s3, s6, s10, s15 = 3.0**0.5, 6.0**0.5, 10.0**0.5, 15.0**0.5
    xx, yy, zz = x * x, y * y, z * z
    return [
        (0, x * 0.0 + 1.0),
        (1, x),
        (1, y),
        (1, z),
        (2, s3 * x * y),
        (2, s3 * y * z),
        (2, s3 * x * z),
        (2, 0.5 * (2.0 * zz - xx - yy)),
        (2, 0.5 * s3 * (xx - yy)),
        (3, 0.5 * z * (2.0 * zz - 3.0 * xx - 3.0 * yy)),
        (3, 0.25 * s6 * x * (4.0 * zz - xx - yy)),
        (3, 0.25 * s6 * y * (4.0 * zz - xx - yy)),
        (3, 0.5 * s15 * z * (xx - yy)),
        (3, s15 * x * y * z),
        (3, 0.25 * s10 * x * (xx - 3.0 * yy)),
        (3, 0.25 * s10 * y * (3.0 * xx - yy)),
    ]


def near_planes():
    slot = np.arange(BOX_DEV * BSIDE * BSIDE)
    box, inner = slot // (BSIDE * BSIDE), slot % (BSIDE * BSIDE)
    row = box // CZ * BSIDE + inner // BSIDE
    col = box % CZ * BSIDE + inner % BSIDE
    gap = np.arange(2 * BSIDE)[:, None, None]
    square = gap**2 + (row[:, None] - row[None]) ** 2 + (col[:, None] - col[None]) ** 2
    radius = np.sqrt(np.maximum(square, 1).astype(np.float64))
    wave = near_scale * np.exp(1j * wave_number * radius) / radius
    wave = np.where(square == 0, self_value, wave)
    return np.concatenate([wave.real, wave.imag], axis=2).astype(ml_dtypes.bfloat16)


def far_terms(slabs):
    lane = np.arange(slabs * 8)
    slab = lane // 16 * 2 + lane % 2
    box = lane // 4 % 4
    part = lane // 2 % 2
    coords = np.stack([slab, box // CZ, box % CZ]).astype(np.float64)
    gap = coords[:, None, :] - coords[:, :, None]
    nearby = np.abs(gap).max(0) < 1.5
    radius = np.sqrt(np.maximum((gap**2).sum(0), 1.0))
    kappa = wave_number * BSIDE
    arg = kappa * radius
    before, now = np.exp(1j * arg) / arg, -1j * np.exp(1j * arg) / arg
    radial = []
    for order in range(4):
        value = (2 * order + 1) * 1j**order * now * far_scale * kappa / 16.0
        radial.append(np.where(nearby, 0.0, value))
        before, now = now, (2 * order + 1) * now / arg - before
    source, target = part[:, None], part[None, :]
    out = np.empty((TERMS, slabs * 8, slabs * 8), ml_dtypes.bfloat16)
    for term, (order, value) in enumerate(harmonics(*(gap / radius))):
        h = radial[order] * value
        cross = np.where(source == 0, h.imag, -h.imag)
        out[term] = np.where(source == target, h.real, cross).astype(ml_dtypes.bfloat16)
    return out


def nt(left, right):
    return lax.dot_general(left, right, (((1,), (1,)), ((), ())), preferred_element_type=F32)


def nn(left, right):
    return lax.dot_general(left, right, (((1,), (0,)), ((), ())), preferred_element_type=F32)


def times_i(x):
    rows = x.shape[0]
    row = lax.broadcasted_iota(jnp.int32, x.shape, 0)
    return jnp.where(row // 2 % 2 == 0, -pltpu.roll(x, rows - 2, 0), pltpu.roll(x, 2, 0))


def kernel(
    n, kdev, kpad, single, inc_ref, con_ref, pos_ref, dir_ref, enc_hbm, dec_hbm, near_hbm, far_hbm,
    one_ref, two_ref, rat_ref,
    enc_v, dec_v, near_v, far_v, own_x, nbr_x, snd, rcv, side_s, side_r, flat,
    load_sem, send_sem, recv_sem, side_ss, side_rs,
):
    me = lax.axis_index("box")
    barrier = pltpu.get_barrier_semaphore()

    def greet(j, carry):
        pl.semaphore_signal(barrier, inc=1, device_id={"box": lax.rem(me + j, n)}, device_id_type=MESH)
        return carry

    lax.fori_loop(1, n, greet, 0, unroll=n <= 32)
    loads = [
        pltpu.make_async_copy(hbm, vmem, load_sem.at[i])
        for i, (hbm, vmem) in enumerate(
            ((enc_hbm, enc_v), (near_hbm, near_v), (far_hbm, far_v), (dec_hbm, dec_v))
        )
    ]
    for load in loads:
        load.start()

    row = lax.broadcasted_iota(jnp.int32, (ROWS, ROWS), 0)
    col = lax.broadcasted_iota(jnp.int32, (ROWS, ROWS), 1)

    def spread(index):
        out = jnp.zeros((ROWS, ROWS), jnp.int32)
        for b in range(BOX_DEV):
            out = jnp.where(index % 4 == b, pos_ref[me * BOX_DEV + b], out)
        return out

    to_grid = jnp.where((row % 4 == col // 4) & (spread(col) == row // 4), 1.0, 0.0).astype(BF16)
    from_grid = jnp.where((col % 4 == row // 4) & (spread(row) == col // 4), 1.0, 0.0).astype(BF16)
    pieces = [inc_ref[a, e].astype(F32) for a in range(2) for e in range(2)]
    field = nn(to_grid, jnp.concatenate(pieces, axis=0).astype(BF16))
    step = con_ref[...].astype(F32) * chi_step
    own_pick = jnp.where((spread(col) == row // 4) & (col < 4), 1.0, 0.0).astype(BF16)
    chi = nn(own_pick, jnp.concatenate([step, jnp.zeros((12, step.shape[1]), F32)], axis=0).astype(BF16))

    drow = lax.broadcasted_iota(jnp.int32, (kpad, kdev), 0)
    dcol = lax.broadcasted_iota(jnp.int32, (kpad, kdev), 1)
    column = [
        jnp.sum(jnp.where(drow == dcol, dir_ref[c : c + 1, :], 0.0), axis=1, keepdims=True)
        for c in range(3)
    ]
    weights = [jnp.concatenate([y, y], axis=0) for _, y in harmonics(*column)]

    lane = lax.broadcasted_iota(jnp.int32, (kpad, LANES), 1)
    even = lane % 2 == 0
    own_x[...] = jnp.zeros_like(own_x)
    nbr_x[...] = jnp.zeros_like(nbr_x)
    if kdev != kpad:
        snd[...] = jnp.zeros_like(snd)
    plane = BSIDE * BSIDE

    def near_sum(ext, low, high):
        total = jnp.zeros((32, 2 * near_v.shape[1]), F32)
        for d in range(low, high):
            if d == 0:
                total += nn(ext[64:96, :].astype(BF16), near_v[0])
            else:
                both = jnp.concatenate([ext[64 + 4 * d : 96 + 4 * d, :], ext[64 - 4 * d : 96 - 4 * d, :]], axis=0)
                got = nn(both.astype(BF16), near_v[d])
                total += got[:32] + got[32:]
        return total

    def exchange(phase):
        def send(j, carry):
            there = lax.rem(me + j, n)
            pltpu.make_async_remote_copy(
                src_ref=snd.at[phase, there],
                dst_ref=rcv.at[phase, me],
                send_sem=send_sem.at[phase],
                recv_sem=recv_sem.at[phase],
                device_id={"box": there},
                device_id_type=MESH,
            ).start()
            return carry

        lax.fori_loop(1, n, send, 0, unroll=n <= 32)
        rcv[phase, pl.ds(me, 1)] = snd[phase, pl.ds(me, 1)]

    def arrived(phase):
        part = rcv.at[phase, pl.ds(0, n - 1)]
        pltpu.make_async_copy(part, part, recv_sem.at[phase]).wait()

    sums = []
    for turn in range(2):
        source = (chi * field).astype(BF16).astype(F32)
        planes = jnp.concatenate(
            [
                jnp.concatenate(
                    [source[4 * g : 4 * g + 4, x * plane : (x + 1) * plane] for g in range(BOX_DEV)], axis=1
                )
                for x in range(BSIDE)
            ],
            axis=0,
        )
        own_x[64:96, :] = planes
        side_s[turn] = planes.astype(BF16)
        if turn == 0:
            pl.semaphore_wait(barrier, n - 1)
        sides = []
        for s, away in enumerate((1, n - 1)):
            sides.append(
                pltpu.make_async_remote_copy(
                    src_ref=side_s.at[turn],
                    dst_ref=side_r.at[turn, s],
                    send_sem=side_ss.at[turn, s],
                    recv_sem=side_rs.at[turn, s],
                    device_id={"box": lax.rem(me + away, n)},
                    device_id_type=MESH,
                )
            )
            sides[-1].start()
        if turn == 0:
            loads[0].wait()
        first = jnp.concatenate([source, jnp.zeros((LANES - ROWS, source.shape[1]), F32)], axis=0)
        second = jnp.concatenate([times_i(source), jnp.zeros((LANES - ROWS, source.shape[1]), F32)], axis=0)
        encoded = nt(enc_v[0], first.astype(BF16)) + nt(enc_v[1], second.astype(BF16))
        if kdev == kpad:
            snd[2 * turn] = encoded.reshape(n, kdev, LANES).astype(BF16)
        else:
            for d in range(n):
                snd[2 * turn, d, :kdev, :] = encoded[d * kdev : (d + 1) * kdev, :].astype(BF16)
        exchange(2 * turn)

        if turn == 0:
            loads[1].wait()
        near = near_sum(own_x, 0, BSIDE)

        arrived(2 * turn)
        columns = [[], []]
        for group in range(n // 16):
            sum0, sum1 = (jnp.zeros((kpad, LANES), F32) for _ in range(2))
            for pair in range(8):
                a = rcv[2 * turn, group * 16 + pair * 2].astype(F32)
                b = rcv[2 * turn, group * 16 + pair * 2 + 1].astype(F32)
                exc0 = jnp.where(even, a, pltpu.roll(b, 1, 1))
                exc1 = jnp.where(even, pltpu.roll(a, LANES - 1, 1), b)
                if pair:
                    exc0, exc1 = pltpu.roll(exc0, 16 * pair, 1), pltpu.roll(exc1, 16 * pair, 1)
                sum0, sum1 = sum0 + exc0, sum1 + exc1
            columns[0].append(sum0)
            columns[1].append(sum1)
        waves = jnp.concatenate([jnp.concatenate(c, axis=1) for c in columns], axis=0).astype(BF16)
        if turn == 0:
            loads[2].wait()
        moved = jnp.zeros((2 * kpad, n * 8), F32)
        for term in range(TERMS):
            moved += weights[term] * nn(waves, far_v[term])
        for group in range(n // 16):
            out0 = moved[:kpad, group * LANES : (group + 1) * LANES]
            out1 = moved[kpad:, group * LANES : (group + 1) * LANES]
            for pair in range(8):
                a, b = out0, out1
                if pair:
                    a, b = pltpu.roll(a, LANES - 16 * pair, 1), pltpu.roll(b, LANES - 16 * pair, 1)
                slab = group * 16 + pair * 2
                snd[2 * turn + 1, slab] = jnp.where(even, a, pltpu.roll(b, 1, 1)).astype(BF16)
                snd[2 * turn + 1, slab + 1] = jnp.where(even, pltpu.roll(a, LANES - 1, 1), b).astype(BF16)
        exchange(2 * turn + 1)

        for side in sides:
            side.wait()
        nbr_x[32:64, :] = jnp.where(me > 0, side_r[turn, 0].astype(F32), 0.0)
        nbr_x[96:128, :] = jnp.where(me < n - 1, side_r[turn, 1].astype(F32), 0.0)
        near = near + near_sum(nbr_x, 1, 2 * BSIDE)
        half = near.shape[1] // 2
        near = near[:, :half] + times_i(near[:, half:])
        near = jnp.concatenate(
            [
                jnp.concatenate(
                    [near[4 * x : 4 * x + 4, g * plane : (g + 1) * plane] for x in range(BSIDE)], axis=1
                )
                for g in range(BOX_DEV)
            ],
            axis=0,
        )

        arrived(2 * turn + 1)
        if kdev == kpad:
            back = rcv[2 * turn + 1].astype(F32).reshape(n * kdev, LANES)
        else:
            for d in range(n):
                flat[d * kdev : (d + 1) * kdev, :] = rcv[2 * turn + 1, d].astype(F32)[:kdev, :]
            back = flat[...]
        back = jnp.transpose(back)[:ROWS]
        if turn == 0:
            loads[3].wait()
        far = nt(back.astype(BF16), dec_v[0]) + nt(times_i(back).astype(BF16), dec_v[1])
        rounded = (near + far).astype(BF16)
        result = nn(from_grid, rounded)
        out_ref = one_ref if turn == 0 else two_ref
        for a in range(2):
            for e in range(2):
                start = (2 * a + e) * BOX_DEV
                out_ref[a, e] = result[start : start + BOX_DEV].astype(BF16)
        field = rounded.astype(F32)
        square = jnp.sum(result * result, axis=1, keepdims=True)
        sums.append(square[:4] + square[4:8] + square[8:12] + square[12:])

    for phase in range(4):
        part = snd.at[phase, pl.ds(0, n - 1)]
        pltpu.make_async_copy(part, part, send_sem.at[phase]).wait()

    count = 4 * inc_ref.shape[3]
    if single:
        values = [jnp.sqrt(sums[1] / count / (sums[0] / count + epsilon))]
    else:
        values = sums
    brow = lax.broadcasted_iota(jnp.int32, (BOX_DEV, 1), 0)
    for i, value in enumerate(values):
        for b in range(BOX_DEV):
            rat_ref[i * BOX_DEV + b] = jnp.sum(jnp.where(brow == b, value, 0.0))


def finish(one_in, two_in, rat_in, one_ref, two_ref, rat_ref):
    one_ref[...] = one_in[...]
    two_ref[...] = two_in[...]
    for b in range(BOX_DEV):
        rat_ref[b] = rat_in[b]


def shards(incident, contrast, box_pos, directions, enc_table, dec_table):
    n = lax.axis_size("box")
    exc_axis = lax.axis_size("exc")
    single = exc_axis == 1
    kdev = directions.shape[1]
    kpad = max(kdev, 16)
    near_np, far_np = near_planes(), far_terms(n)
    vmem = pl.BlockSpec(memory_space=pltpu.VMEM)
    smem = pl.BlockSpec(memory_space=pltpu.SMEM)
    anyspace = pl.BlockSpec(memory_space=pl.ANY)
    width = near_np.shape[1]
    one, two, ratio = pl.pallas_call(
        functools.partial(kernel, n, kdev, kpad, single),
        out_shape=(
            jax.ShapeDtypeStruct(incident.shape, BF16),
            jax.ShapeDtypeStruct(incident.shape, BF16),
            jax.ShapeDtypeStruct((BOX_DEV if single else 2 * BOX_DEV,), F32),
        ),
        in_specs=[vmem, vmem, smem, vmem, anyspace, anyspace, anyspace, anyspace],
        out_specs=(vmem, vmem, smem),
        scratch_shapes=[
            pltpu.VMEM(enc_table.shape, BF16),
            pltpu.VMEM(dec_table.shape, BF16),
            pltpu.VMEM(near_np.shape, BF16),
            pltpu.VMEM(far_np.shape, BF16),
            pltpu.VMEM((160, width), F32),
            pltpu.VMEM((160, width), F32),
            pltpu.VMEM((4, n, kpad, LANES), BF16),
            pltpu.VMEM((4, n, kpad, LANES), BF16),
            pltpu.VMEM((2, 32, width), BF16),
            pltpu.VMEM((2, 2, 32, width), BF16),
            pltpu.VMEM((n * kdev, LANES), F32),
            pltpu.SemaphoreType.DMA((4,)),
            pltpu.SemaphoreType.DMA((4,)),
            pltpu.SemaphoreType.DMA((4,)),
            pltpu.SemaphoreType.DMA((2, 2)),
            pltpu.SemaphoreType.DMA((2, 2)),
        ],
        compiler_params=pltpu.CompilerParams(
            collective_id=0, has_side_effects=True, vmem_limit_bytes=56 * 1024 * 1024
        ),
    )(
        incident, contrast, box_pos, directions, enc_table, dec_table, jnp.asarray(near_np), jnp.asarray(far_np)
    )
    if not single:
        sums = lax.psum(ratio.reshape(2, BOX_DEV), "exc")
        count = 4 * incident.shape[3] * exc_axis
        ratio = jnp.sqrt(sums[1] / count / (sums[0] / count + epsilon))
    return pl.pallas_call(
        finish,
        out_shape=[jax.ShapeDtypeStruct(x.shape, x.dtype) for x in (one, two, ratio)],
        in_specs=[vmem, vmem, smem],
        out_specs=[vmem, vmem, smem],
    )(one, two, ratio)


def solution(mesh):
    placed = (P(None, "exc", "box", None), P("box", None), P(), P(None, "box"), P(), P())
    return jax.shard_map(
        shards,
        mesh=mesh,
        in_specs=placed,
        out_specs=(P(None, "exc", "box", None), P(None, "exc", "box", None), P("box")),
        check_vma=False,
    )
```

```python
import functools

import jax
import jax.numpy as jnp
import ml_dtypes
import numpy as np
from jax import lax
from jax.experimental import pallas as pl
from jax.experimental.pallas import tpu as pltpu
from jax.sharding import PartitionSpec as P

BSIDE = 8
CY = 2
CZ = 2
BOX_DEV = CY * CZ
ROWS = 4 * BOX_DEV
LANES = 128
TERMS = 16
MESH = pl.DeviceIdType.MESH

wave_number = 0.8
near_scale = 0.1
self_value = 1.0
far_scale = 0.25
chi_step = 0.0625
epsilon = 1e-06

F32 = jnp.float32
BF16 = jnp.bfloat16


def harmonics(x, y, z):
    s3, s6, s10, s15 = 3.0**0.5, 6.0**0.5, 10.0**0.5, 15.0**0.5
    xx, yy, zz = x * x, y * y, z * z
    return [
        (0, x * 0.0 + 1.0),
        (1, x),
        (1, y),
        (1, z),
        (2, s3 * x * y),
        (2, s3 * y * z),
        (2, s3 * x * z),
        (2, 0.5 * (2.0 * zz - xx - yy)),
        (2, 0.5 * s3 * (xx - yy)),
        (3, 0.5 * z * (2.0 * zz - 3.0 * xx - 3.0 * yy)),
        (3, 0.25 * s6 * x * (4.0 * zz - xx - yy)),
        (3, 0.25 * s6 * y * (4.0 * zz - xx - yy)),
        (3, 0.5 * s15 * z * (xx - yy)),
        (3, s15 * x * y * z),
        (3, 0.25 * s10 * x * (xx - 3.0 * yy)),
        (3, 0.25 * s10 * y * (3.0 * xx - yy)),
    ]


def near_planes():
    slot = np.arange(BOX_DEV * BSIDE * BSIDE)
    box, inner = slot // (BSIDE * BSIDE), slot % (BSIDE * BSIDE)
    row = box // CZ * BSIDE + inner // BSIDE
    col = box % CZ * BSIDE + inner % BSIDE
    gap = np.arange(2 * BSIDE)[:, None, None]
    square = gap**2 + (row[:, None] - row[None]) ** 2 + (col[:, None] - col[None]) ** 2
    radius = np.sqrt(np.maximum(square, 1).astype(np.float64))
    wave = near_scale * np.exp(1j * wave_number * radius) / radius
    wave = np.where(square == 0, self_value, wave)
    return np.concatenate([wave.real, wave.imag], axis=2).astype(ml_dtypes.bfloat16)


def far_terms(slabs):
    lane = np.arange(slabs * 8)
    slab = lane // 16 * 2 + lane % 2
    box = lane // 4 % 4
    part = lane // 2 % 2
    coords = np.stack([slab, box // CZ, box % CZ]).astype(np.float64)
    gap = coords[:, None, :] - coords[:, :, None]
    nearby = np.abs(gap).max(0) < 1.5
    radius = np.sqrt(np.maximum((gap**2).sum(0), 1.0))
    kappa = wave_number * BSIDE
    arg = kappa * radius
    before, now = np.exp(1j * arg) / arg, -1j * np.exp(1j * arg) / arg
    radial = []
    for order in range(4):
        value = (2 * order + 1) * 1j**order * now * far_scale * kappa / 16.0
        radial.append(np.where(nearby, 0.0, value))
        before, now = now, (2 * order + 1) * now / arg - before
    source, target = part[:, None], part[None, :]
    out = np.empty((TERMS, slabs * 8, slabs * 8), ml_dtypes.bfloat16)
    for term, (order, value) in enumerate(harmonics(*(gap / radius))):
        h = radial[order] * value
        cross = np.where(source == 0, h.imag, -h.imag)
        out[term] = np.where(source == target, h.real, cross).astype(ml_dtypes.bfloat16)
    return out


def nt(left, right):
    return lax.dot_general(left, right, (((1,), (1,)), ((), ())), preferred_element_type=F32)


def nn(left, right):
    return lax.dot_general(left, right, (((1,), (0,)), ((), ())), preferred_element_type=F32)


def times_i(x):
    rows = x.shape[0]
    row = lax.broadcasted_iota(jnp.int32, x.shape, 0)
    return jnp.where(row // 2 % 2 == 0, -pltpu.roll(x, rows - 2, 0), pltpu.roll(x, 2, 0))


def kernel(
    n, kdev, kpad, single, inc_ref, con_ref, pos_ref, dir_ref, enc_hbm, dec_hbm, near_hbm, far_hbm,
    one_ref, two_ref, rat_ref,
    enc_v, dec_v, near_v, far_v, own_x, nbr_x, snd, rcv, side_s, side_r, flat,
    load_sem, send_sem, recv_sem, side_ss, side_rs,
):
    me = lax.axis_index("box")
    barrier = pltpu.get_barrier_semaphore()

    def greet(j, carry):
        pl.semaphore_signal(barrier, inc=1, device_id={"box": lax.rem(me + j, n)}, device_id_type=MESH)
        return carry

    lax.fori_loop(1, n, greet, 0, unroll=n <= 32)
    loads = [
        pltpu.make_async_copy(hbm, vmem, load_sem.at[i])
        for i, (hbm, vmem) in enumerate(
            ((enc_hbm, enc_v), (near_hbm, near_v), (far_hbm, far_v), (dec_hbm, dec_v))
        )
    ]
    for load in loads:
        load.start()

    row = lax.broadcasted_iota(jnp.int32, (ROWS, ROWS), 0)
    col = lax.broadcasted_iota(jnp.int32, (ROWS, ROWS), 1)

    def spread(index):
        out = jnp.zeros((ROWS, ROWS), jnp.int32)
        for b in range(BOX_DEV):
            out = jnp.where(index % 4 == b, pos_ref[me * BOX_DEV + b], out)
        return out

    to_grid = jnp.where((row % 4 == col // 4) & (spread(col) == row // 4), 1.0, 0.0).astype(BF16)
    from_grid = jnp.where((col % 4 == row // 4) & (spread(row) == col // 4), 1.0, 0.0).astype(BF16)
    pieces = [inc_ref[a, e].astype(F32) for a in range(2) for e in range(2)]
    field = nn(to_grid, jnp.concatenate(pieces, axis=0).astype(BF16))
    step = con_ref[...].astype(F32) * chi_step
    own_pick = jnp.where((spread(col) == row // 4) & (col < 4), 1.0, 0.0).astype(BF16)
    chi = nn(own_pick, jnp.concatenate([step, jnp.zeros((12, step.shape[1]), F32)], axis=0).astype(BF16))

    drow = lax.broadcasted_iota(jnp.int32, (kpad, kdev), 0)
    dcol = lax.broadcasted_iota(jnp.int32, (kpad, kdev), 1)
    column = [
        jnp.sum(jnp.where(drow == dcol, dir_ref[c : c + 1, :], 0.0), axis=1, keepdims=True)
        for c in range(3)
    ]
    weights = [jnp.concatenate([y, y], axis=0) for _, y in harmonics(*column)]

    lane = lax.broadcasted_iota(jnp.int32, (kpad, LANES), 1)
    even = lane % 2 == 0
    own_x[...] = jnp.zeros_like(own_x)
    nbr_x[...] = jnp.zeros_like(nbr_x)
    if kdev != kpad:
        snd[...] = jnp.zeros_like(snd)
    plane = BSIDE * BSIDE

    direction = lax.broadcasted_iota(jnp.int32, (kpad, LANES), 0)
    mine = direction % 8 == lane // ROWS

    def pack(x):
        if kdev != kpad:
            return x.astype(BF16)
        x = jnp.where(mine, x, 0.0)
        return jnp.concatenate([jnp.sum(x[h : h + 8], axis=0, keepdims=True) for h in range(0, kpad, 8)], axis=0)

    def unpack(x):
        if kdev != kpad:
            return jnp.where(lane < ROWS, x, 0.0)
        rows = [jnp.broadcast_to(x[h : h + 1], (8, LANES)) for h in range(kpad // 8)]
        return jnp.where(mine, jnp.concatenate(rows, axis=0), 0.0)

    def stagger(x, shift):
        if kdev != kpad:
            return x
        out = x
        for j in range(1, 8):
            out = jnp.where(direction % 8 == j, pltpu.roll(x, shift * j % LANES, 1), out)
        return out

    def near_sum(ext, low, high):
        total = jnp.zeros((32, 2 * near_v.shape[1]), F32)
        for d in range(low, high):
            if d == 0:
                total += nn(ext[64:96, :].astype(BF16), near_v[0])
            else:
                both = jnp.concatenate([ext[64 + 4 * d : 96 + 4 * d, :], ext[64 - 4 * d : 96 - 4 * d, :]], axis=0)
                got = nn(both.astype(BF16), near_v[d])
                total += got[:32] + got[32:]
        return total

    def exchange(phase):
        def send(j, carry):
            there = lax.rem(me + j, n)
            pltpu.make_async_remote_copy(
                src_ref=snd.at[phase, there],
                dst_ref=rcv.at[phase, me],
                send_sem=send_sem.at[phase],
                recv_sem=recv_sem.at[phase],
                device_id={"box": there},
                device_id_type=MESH,
            ).start()
            return carry

        lax.fori_loop(1, n, send, 0, unroll=n <= 32)
        rcv[phase, pl.ds(me, 1)] = snd[phase, pl.ds(me, 1)]

    def arrived(phase):
        part = rcv.at[phase, pl.ds(0, n - 1)]
        pltpu.make_async_copy(part, part, recv_sem.at[phase]).wait()

    sums = []
    for turn in range(2):
        source = (chi * field).astype(BF16).astype(F32)
        planes = jnp.concatenate(
            [
                jnp.concatenate(
                    [source[4 * g : 4 * g + 4, x * plane : (x + 1) * plane] for g in range(BOX_DEV)], axis=1
                )
                for x in range(BSIDE)
            ],
            axis=0,
        )
        own_x[64:96, :] = planes
        side_s[turn] = planes.astype(BF16)
        if turn == 0:
            pl.semaphore_wait(barrier, n - 1)
        sides = []
        for s, away in enumerate((1, n - 1)):
            sides.append(
                pltpu.make_async_remote_copy(
                    src_ref=side_s.at[turn],
                    dst_ref=side_r.at[turn, s],
                    send_sem=side_ss.at[turn, s],
                    recv_sem=side_rs.at[turn, s],
                    device_id={"box": lax.rem(me + away, n)},
                    device_id_type=MESH,
                )
            )
            sides[-1].start()
        if turn == 0:
            loads[0].wait()
        first = jnp.concatenate([source] * (LANES // ROWS), axis=0)
        second = jnp.concatenate([times_i(source)] * (LANES // ROWS), axis=0)
        encoded = nt(enc_v[0], first.astype(BF16)) + nt(enc_v[1], second.astype(BF16))
        if kdev == kpad:
            for d in range(n):
                snd[2 * turn, d] = pack(encoded[d * kdev : (d + 1) * kdev, :])
        else:
            for d in range(n):
                snd[2 * turn, d, :kdev, :] = encoded[d * kdev : (d + 1) * kdev, :].astype(BF16)
        exchange(2 * turn)

        if turn == 0:
            loads[1].wait()
        near = near_sum(own_x, 0, BSIDE)

        arrived(2 * turn)
        columns = [[], []]
        for group in range(n // 16):
            sum0, sum1 = (jnp.zeros((kpad, LANES), F32) for _ in range(2))
            for pair in range(8):
                a = unpack(rcv[2 * turn, group * 16 + pair * 2].astype(F32))
                b = unpack(rcv[2 * turn, group * 16 + pair * 2 + 1].astype(F32))
                exc0 = jnp.where(even, a, pltpu.roll(b, 1, 1))
                exc1 = jnp.where(even, pltpu.roll(a, LANES - 1, 1), b)
                if pair:
                    exc0, exc1 = pltpu.roll(exc0, 16 * pair, 1), pltpu.roll(exc1, 16 * pair, 1)
                sum0, sum1 = sum0 + exc0, sum1 + exc1
            columns[0].append(stagger(sum0, LANES - ROWS))
            columns[1].append(stagger(sum1, LANES - ROWS))
        waves = jnp.concatenate([jnp.concatenate(c, axis=1) for c in columns], axis=0).astype(BF16)
        if turn == 0:
            loads[2].wait()
        moved = jnp.zeros((2 * kpad, n * 8), F32)
        for term in range(TERMS):
            moved += weights[term] * nn(waves, far_v[term])
        for group in range(n // 16):
            out0 = stagger(moved[:kpad, group * LANES : (group + 1) * LANES], ROWS)
            out1 = stagger(moved[kpad:, group * LANES : (group + 1) * LANES], ROWS)
            for pair in range(8):
                a, b = out0, out1
                if pair:
                    a, b = pltpu.roll(a, LANES - 16 * pair, 1), pltpu.roll(b, LANES - 16 * pair, 1)
                slab = group * 16 + pair * 2
                snd[2 * turn + 1, slab] = pack(jnp.where(even, a, pltpu.roll(b, 1, 1)))
                snd[2 * turn + 1, slab + 1] = pack(jnp.where(even, pltpu.roll(a, LANES - 1, 1), b))
        exchange(2 * turn + 1)

        for side in sides:
            side.wait()
        nbr_x[32:64, :] = jnp.where(me > 0, side_r[turn, 0].astype(F32), 0.0)
        nbr_x[96:128, :] = jnp.where(me < n - 1, side_r[turn, 1].astype(F32), 0.0)
        near = near + near_sum(nbr_x, 1, 2 * BSIDE)
        half = near.shape[1] // 2
        near = near[:, :half] + times_i(near[:, half:])
        near = jnp.concatenate(
            [
                jnp.concatenate(
                    [near[4 * x : 4 * x + 4, g * plane : (g + 1) * plane] for x in range(BSIDE)], axis=1
                )
                for g in range(BOX_DEV)
            ],
            axis=0,
        )

        arrived(2 * turn + 1)
        if kdev == kpad:
            back = jnp.concatenate([unpack(rcv[2 * turn + 1, d]) for d in range(n)], axis=0)
        else:
            for d in range(n):
                flat[d * kdev : (d + 1) * kdev, :] = rcv[2 * turn + 1, d].astype(F32)[:kdev, :]
            back = flat[...]
        back = jnp.transpose(back)
        if kdev == kpad:
            back = sum(back[c * ROWS : (c + 1) * ROWS] for c in range(LANES // ROWS))
        else:
            back = back[:ROWS]
        if turn == 0:
            loads[3].wait()
        far = nt(back.astype(BF16), dec_v[0]) + nt(times_i(back).astype(BF16), dec_v[1])
        rounded = (near + far).astype(BF16)
        result = nn(from_grid, rounded)
        out_ref = one_ref if turn == 0 else two_ref
        for a in range(2):
            for e in range(2):
                start = (2 * a + e) * BOX_DEV
                out_ref[a, e] = result[start : start + BOX_DEV].astype(BF16)
        field = rounded.astype(F32)
        square = jnp.sum(result * result, axis=1, keepdims=True)
        sums.append(square[:4] + square[4:8] + square[8:12] + square[12:])

    for phase in range(4):
        part = snd.at[phase, pl.ds(0, n - 1)]
        pltpu.make_async_copy(part, part, send_sem.at[phase]).wait()

    count = 4 * inc_ref.shape[3]
    if single:
        values = [jnp.sqrt(sums[1] / count / (sums[0] / count + epsilon))]
    else:
        values = sums
    brow = lax.broadcasted_iota(jnp.int32, (BOX_DEV, 1), 0)
    for i, value in enumerate(values):
        for b in range(BOX_DEV):
            rat_ref[i * BOX_DEV + b] = jnp.sum(jnp.where(brow == b, value, 0.0))


def finish(one_in, two_in, rat_in, one_ref, two_ref, rat_ref):
    one_ref[...] = one_in[...]
    two_ref[...] = two_in[...]
    for b in range(BOX_DEV):
        rat_ref[b] = rat_in[b]


def shards(incident, contrast, box_pos, directions, enc_table, dec_table):
    n = lax.axis_size("box")
    exc_axis = lax.axis_size("exc")
    single = exc_axis == 1
    kdev = directions.shape[1]
    kpad = max(kdev, 16)
    near_np, far_np = near_planes(), far_terms(n)
    vmem = pl.BlockSpec(memory_space=pltpu.VMEM)
    smem = pl.BlockSpec(memory_space=pltpu.SMEM)
    anyspace = pl.BlockSpec(memory_space=pl.ANY)
    width = near_np.shape[1]
    message = ((4, n, kpad // 8, LANES), F32) if kdev == kpad else ((4, n, kpad, LANES), BF16)
    one, two, ratio = pl.pallas_call(
        functools.partial(kernel, n, kdev, kpad, single),
        out_shape=(
            jax.ShapeDtypeStruct(incident.shape, BF16),
            jax.ShapeDtypeStruct(incident.shape, BF16),
            jax.ShapeDtypeStruct((BOX_DEV if single else 2 * BOX_DEV,), F32),
        ),
        in_specs=[vmem, vmem, smem, vmem, anyspace, anyspace, anyspace, anyspace],
        out_specs=(vmem, vmem, smem),
        scratch_shapes=[
            pltpu.VMEM(enc_table.shape, BF16),
            pltpu.VMEM(dec_table.shape, BF16),
            pltpu.VMEM(near_np.shape, BF16),
            pltpu.VMEM(far_np.shape, BF16),
            pltpu.VMEM((160, width), F32),
            pltpu.VMEM((160, width), F32),
            pltpu.VMEM(*message),
            pltpu.VMEM(*message),
            pltpu.VMEM((2, 32, width), BF16),
            pltpu.VMEM((2, 2, 32, width), BF16),
            pltpu.VMEM((n * kdev, LANES), F32),
            pltpu.SemaphoreType.DMA((4,)),
            pltpu.SemaphoreType.DMA((4,)),
            pltpu.SemaphoreType.DMA((4,)),
            pltpu.SemaphoreType.DMA((2, 2)),
            pltpu.SemaphoreType.DMA((2, 2)),
        ],
        compiler_params=pltpu.CompilerParams(
            collective_id=0, has_side_effects=True, vmem_limit_bytes=56 * 1024 * 1024
        ),
    )(
        incident, contrast, box_pos, directions, enc_table, dec_table, jnp.asarray(near_np), jnp.asarray(far_np)
    )
    if not single:
        sums = lax.psum(ratio.reshape(2, BOX_DEV), "exc")
        count = 4 * incident.shape[3] * exc_axis
        ratio = jnp.sqrt(sums[1] / count / (sums[0] / count + epsilon))
    return pl.pallas_call(
        finish,
        out_shape=[jax.ShapeDtypeStruct(x.shape, x.dtype) for x in (one, two, ratio)],
        in_specs=[vmem, vmem, smem],
        out_specs=[vmem, vmem, smem],
    )(one, two, ratio)


def solution(mesh):
    placed = (P(None, "exc", "box", None), P("box", None), P(), P(None, "box"), P(), P())
    return jax.shard_map(
        shards,
        mesh=mesh,
        in_specs=placed,
        out_specs=(P(None, "exc", "box", None), P(None, "exc", "box", None), P("box")),
        check_vma=False,
    )
```
